256 devices in a mesh: tm: 32 (over x, y, core), rows: 8 (over z).
Axes of the slice: x: 4, y: 4, z: 8, core: 2. Of those that a mesh axis runs over, the one named last changes fastest.
Arguments:
- latent: bfloat16 [32, 64, 128, 256], P('tm', 'rows'), may hold values from -6 to 6
- gain_one: float32 [256], replicated, may hold values from 0.1 to 1.9
- conv_one: bfloat16 [3, 3, 3, 256, 256], replicated, may hold values from -0.078125 to 0.078125
- gain_two: float32 [256], replicated, may hold values from 0.1 to 1.9
- conv_two: bfloat16 [3, 3, 3, 256, 256], replicated, may hold values from -0.078125 to 0.078125
- up_weight: bfloat16 [3, 3, 256, 128], replicated, may hold values from -0.125 to 0.125
Outputs:
- upsampled: bfloat16 [32, 128, 256, 128], P('tm', 'rows')
The draws below stay inside these ranges and needn't reach their ends.
All inputs are finite; a program needn't handle non-finite values.
Results may differ from the reference program's by a relative error of at most 0.0054.
Values may be sent and summed in bfloat16 or wider, within the bound.
A program may use at most 64 MiB of HBM per device.

```python
import jax
import jax.numpy as jnp
from jax import lax

C = 256
COUT = 128
W = 128
FRAMES = 32
ROWS = 64


def steps_of(own_key, extent, shards, least, largest):
    loudness = 1.0
    for dim, shards_of in shards:
        heights = jax.random.uniform(jax.random.fold_in(jax.random.fold_in(own_key, 6), dim), (shards_of,), jnp.float32, least / len(shards), largest / len(shards))
        loudness = loudness * jnp.repeat(jnp.exp(heights), extent[dim] // shards_of).reshape((-1,) + (1,) * (len(extent) - 1 - dim))
    return loudness


def gaussian(own_key, shape, width, bound, pieces=(), kind=jnp.bfloat16):
    values = width * jax.random.normal(own_key, shape, jnp.float32)
    if pieces:
        values = values * steps_of(own_key, shape, pieces, -0.22, 0.18)
    return jnp.clip(values, -bound, bound).astype(kind)


def setup_inputs(seed: int = 0) -> dict:
    splits = jax.random.split(jax.random.key(seed), 7)
    return {
        "latent": gaussian(splits[0], (FRAMES, ROWS, W, C), 1.0, 6.0, ((0, 32), (1, 8))),
        "gain_one": jnp.clip(1.0 + 0.18 * jax.random.normal(splits[1], (C,), jnp.float32), 0.1, 1.9),
        "conv_one": gaussian(splits[2], (3, 3, 3, C, C), (27 * C) ** -0.5, 0.078125),
        "gain_two": jnp.clip(1.0 + 0.18 * jax.random.normal(splits[3], (C,), jnp.float32), 0.1, 1.9),
        "conv_two": gaussian(splits[4], (3, 3, 3, C, C), (27 * C) ** -0.5, 0.078125),
        "up_weight": gaussian(splits[5], (3, 3, C, COUT), (9 * C) ** -0.5, 0.125),
    }


def norm_silu(values, scales):
    mean_sq = lax.optimization_barrier(jnp.mean(values * values, axis=-1, keepdims=True))
    return jax.nn.silu(values * lax.rsqrt(mean_sq + 1e-06) * scales)

def causal(hidden, kernel):
    padded = jnp.pad(hidden.astype(jnp.float32), ((2, 0), (1, 1), (1, 1), (0, 0)))
    result = lax.conv_general_dilated(padded[None], kernel.astype(jnp.float32), (1, 1, 1), 'VALID', dimension_numbers=('NDHWC', 'DHWIO', 'NDHWC'), precision=lax.Precision.HIGHEST)
    return result[0]

def reference(latent, gain_one, conv_one, gain_two, conv_two, up_weight):
    source = latent.astype(jnp.float32)
    first = norm_silu(source, gain_one).astype(jnp.bfloat16)
    inner = causal(first, conv_one)
    second = norm_silu(inner, gain_two).astype(jnp.bfloat16)
    block_out = (source + causal(second, conv_two)).astype(jnp.bfloat16)
    kernel = up_weight.astype(jnp.float32)

    def one_frame(frame):
        grown = jnp.repeat(jnp.repeat(frame, 2, axis=0), 2, axis=1).astype(jnp.float32)
        grown = jnp.pad(grown, ((1, 1), (1, 1), (0, 0)))
        result = lax.conv_general_dilated(grown[None], kernel, (1, 1), 'VALID', dimension_numbers=('NHWC', 'HWIO', 'NHWC'), precision=lax.Precision.HIGHEST)
        return result[0].astype(jnp.bfloat16)
    return lax.map(one_frame, block_out)
```

```python
import functools

import jax
import jax.numpy as jnp
from jax import lax
from jax.experimental import pallas as pl
from jax.experimental.pallas import tpu as pltpu
from jax.sharding import PartitionSpec as P

MESH = pl.DeviceIdType.MESH
PAD = 8


def windows(width, first, step):
    edges = [0, first]
    while edges[-1] < width:
        edges.append(min(edges[-1] + step, width))
    return list(zip(edges[:-1], edges[1:]))


def settled(wins, width, lag):
    edges = [0] + [max(hi - lag, 0) for _, hi in wins[:-1]] + [width]
    return list(zip(edges[:-1], edges[1:]))


def norm_silu(values, scales):
    mean_sq = jnp.mean(values * values, axis=-1, keepdims=True)
    u = values * lax.rsqrt(mean_sq + 1e-06) * scales
    return 0.5 * u * (1.0 + jnp.tanh(0.5 * u))


def kernel(
    sizes,
    wins,
    latent,
    gain_one,
    gain_two,
    conv_one,
    conv_two,
    up_weight,
    out,
    lat,
    weights,
    up_raw,
    up_mat,
    held,
    block,
    sums,
    up_sums,
    woven,
    packed,
    load_sem,
    out_sem,
    frame_send,
    frame_recv,
    pair_send,
    pair_recv,
    rim_send,
    rim_recv,
    edge_send,
    edge_recv,
):
    frames, bands = sizes
    height, width, channels = lat.shape
    growth = up_raw.shape[3]
    tm, rw = lax.axis_index("tm"), lax.axis_index("rows")
    odd = lax.rem(tm, 2)
    mate = (tm + 1 - 2 * odd, rw)
    ahead = (lax.rem(tm + 2, frames), rw)
    behind = (lax.rem(tm + frames - 2, frames), rw)
    above = (tm, lax.rem(rw + bands - 1, bands))
    below = (tm, lax.rem(rw + 1, bands))
    body = pl.ds(1, height)

    loads = [pltpu.make_async_copy(latent.at[0], lat, load_sem.at[0])]
    for stage, conv in enumerate((conv_one, conv_two)):
        for e in range(3):
            loads.append(
                pltpu.make_async_copy(
                    conv.at[:, :, e], weights.at[stage, e], load_sem.at[1 + 3 * stage + e]
                )
            )
    loads.append(pltpu.make_async_copy(up_weight, up_raw, load_sem.at[7]))
    for load in loads:
        load.start()

    barrier = pltpu.get_barrier_semaphore()
    for peer in (behind, mate, above, below):
        pl.semaphore_signal(barrier, inc=1, device_id=peer, device_id_type=MESH)

    def remote(src, dst, send, recv, peer):
        return pltpu.make_async_remote_copy(
            src_ref=src, dst_ref=dst, send_sem=send, recv_sem=recv, device_id=peer, device_id_type=MESH
        )

    def to_ahead(s, c):
        cols = pl.ds(wins[s][c][0], wins[s][c][1] - wins[s][c][0])
        return remote(
            held.at[s, 2, body, cols],
            held.at[s, 0, body, cols],
            frame_send.at[s, c],
            frame_recv.at[s, c],
            ahead,
        )

    def to_mate(s, c):
        cols = pl.ds(wins[s][c][0], wins[s][c][1] - wins[s][c][0])
        return remote(
            held.at[s, 2 - 2 * odd, body, cols],
            held.at[s, 1, body, cols],
            pair_send.at[s, c],
            pair_recv.at[s, c],
            mate,
        )

    def to_rims(s, c):
        cols = pl.ds(wins[s][c][0], wins[s][c][1] - wins[s][c][0])
        return [
            remote(
                held.at[s, :, mine, cols],
                held.at[s, :, theirs, cols],
                rim_send.at[s, c, k],
                rim_recv.at[s, c, k],
                peer,
            )
            for k, (mine, theirs, peer) in enumerate(((1, height + 1, above), (height, 0, below)))
        ]

    def to_edges(c):
        cols = pl.ds(wins[2][c][0], wins[2][c][1] - wins[2][c][0])
        return [
            remote(
                block.at[mine, cols],
                block.at[theirs, cols],
                edge_send.at[c, k],
                edge_recv.at[c, k],
                peer,
            )
            for k, (mine, theirs, peer) in enumerate(((1, height + 1, above), (height, 0, below)))
        ]

    def take_frame(s, c):
        lo, hi = wins[s][c]
        to_ahead(s, c).wait_recv()

        @pl.when(tm < 2)
        def _():
            held[s, 0, 1 : height + 1, lo:hi] = jnp.zeros((height, hi - lo, channels), held.dtype)

        to_mate(s, c).start()

    def take_pair(s, c):
        to_mate(s, c).wait_recv()
        for copy in to_rims(s, c):
            copy.start()

    def take_rims(s, c):
        lo, hi = wins[s][c]
        for copy in to_rims(s, c):
            copy.wait_recv()
        blank = jnp.zeros((3, hi - lo, channels), held.dtype)

        @pl.when(rw == 0)
        def _():
            held[s, :, 0, lo:hi] = blank

        @pl.when(rw == bands - 1)
        def _():
            held[s, :, height + 1, lo:hi] = blank

    def multiply(s, c):
        lo, hi = wins[s][c]
        rows = height * (hi - lo)
        left = jnp.concatenate(
            [
                held[s, a, b : b + height, lo:hi].reshape(rows, channels)
                for a in range(3)
                for b in range(3)
            ],
            axis=1,
        )
        for e in range(3):
            term = jnp.dot(
                left,
                weights[s, e].reshape(9 * channels, channels),
                preferred_element_type=jnp.float32,
            )
            sums[e, :, PAD + lo : PAD + hi] = term.reshape(height, hi - lo, channels)

    def total(r, lo, hi):
        return (
            sums[0, r, PAD + lo - 1 : PAD + hi - 1]
            + sums[1, r, PAD + lo : PAD + hi]
            + sums[2, r, PAD + lo + 1 : PAD + hi + 1]
        )

    def settle_one(c):
        lo, hi = wins[1][c]

        def row(r, _):
            held[1, 2, 1 + r, lo:hi] = norm_silu(total(r, lo, hi), gain_two[...]).astype(held.dtype)
            return 0

        lax.fori_loop(0, height, row, 0)
        to_ahead(1, c).start()

    def settle_two(c):
        lo, hi = wins[2][c]

        def row(r, _):
            value = lat[r, lo:hi].astype(jnp.float32) + total(r, lo, hi)
            block[1 + r, lo:hi] = value.astype(block.dtype)
            return 0

        lax.fori_loop(0, height, row, 0)
        for copy in to_edges(c):
            copy.start()

    def upsample(c):
        lo, hi = wins[2][c]
        for copy in to_edges(c):
            copy.wait_recv()
        blank = jnp.zeros((hi - lo, channels), block.dtype)

        @pl.when(rw == 0)
        def _():
            block[0, lo:hi] = blank

        @pl.when(rw == bands - 1)
        def _():
            block[height + 1, lo:hi] = blank

        rows = height * (hi - lo)
        for p in range(2):
            left = jnp.concatenate(
                [block[p + d : p + d + height, lo:hi].reshape(rows, channels) for d in range(2)], axis=1
            )
            term = jnp.dot(left, up_mat[p], preferred_element_type=jnp.float32)
            up_sums[p, :, PAD + lo : PAD + hi] = term.reshape(height, hi - lo, 4 * growth)

    def weave(c):
        lo, hi = wins[3][c]
        n = hi - lo
        if n == 0:
            return
        g = growth

        def row(r, _):
            for p in range(2):
                even = (
                    up_sums[p, r, PAD + lo - 1 : PAD + hi - 1, 0:g]
                    + up_sums[p, r, PAD + lo : PAD + hi, g : 2 * g]
                )
                odds = (
                    up_sums[p, r, PAD + lo : PAD + hi, 2 * g : 3 * g]
                    + up_sums[p, r, PAD + lo + 1 : PAD + hi + 1, 3 * g : 4 * g]
                )
                woven[pl.ds(0, n, stride=2), :] = even
                woven[pl.ds(1, n, stride=2), :] = odds
                packed[2 * r + p, 2 * lo : 2 * hi] = woven[0 : 2 * n, :].astype(packed.dtype)
            return 0

        lax.fori_loop(0, height, row, 0)
        to_out(c).start()

    def to_out(c):
        lo, hi = wins[3][c]
        cols = pl.ds(2 * lo, 2 * (hi - lo))
        return pltpu.make_async_copy(packed.at[:, cols], out.at[0, :, cols], out_sem.at[c])

    loads[0].wait()
    pl.semaphore_wait(barrier, 4)
    for c, (lo, hi) in enumerate(wins[0]):

        def row(r, _, lo=lo, hi=hi):
            value = lat[r, lo:hi].astype(jnp.float32)
            held[0, 2, 1 + r, lo:hi] = norm_silu(value, gain_one[...]).astype(held.dtype)
            return 0

        lax.fori_loop(0, height, row, 0)
        to_ahead(0, c).start()

    sums[0, :, 0:PAD] = jnp.zeros((height, PAD, channels), jnp.float32)
    sums[2, :, PAD + width :] = jnp.zeros((height, PAD, channels), jnp.float32)
    for p in range(2):
        up_sums[p, :, 0:PAD, 0:growth] = jnp.zeros((height, PAD, growth), jnp.float32)
        up_sums[p, :, PAD + width :, 3 * growth :] = jnp.zeros((height, PAD, growth), jnp.float32)
    loads[7].wait()
    for p, groups in enumerate((((0,), (1, 2)), ((0, 1), (2,)))):
        for d, group in enumerate(groups):
            col = [sum(up_raw[b, e].astype(jnp.float32) for b in group) for e in range(3)]
            parts = (col[0], col[1] + col[2], col[0] + col[1], col[2])
            for k, part in enumerate(parts):
                up_mat[p, d * channels : (d + 1) * channels, k * growth : (k + 1) * growth] = part.astype(
                    up_mat.dtype
                )

    count = len(wins[0])
    take_frame(0, 0)
    take_pair(0, 0)
    for load in loads[1:4]:
        load.wait()
    for c in range(count):
        if c + 1 < count:
            take_frame(0, c + 1)
        take_rims(0, c)
        multiply(0, c)
        settle_one(c)
        if c + 1 < count:
            take_pair(0, c + 1)

    count = len(wins[1])
    take_frame(1, 0)
    take_pair(1, 0)
    for load in loads[4:7]:
        load.wait()
    for c in range(count):
        if c + 1 < count:
            take_frame(1, c + 1)
        take_rims(1, c)
        multiply(1, c)
        settle_two(c)
        if c + 1 < count:
            take_pair(1, c + 1)
        if c > 0:
            upsample(c - 1)
            weave(c - 1)
    upsample(count - 1)
    weave(count - 1)

    for s in range(2):
        for c in range(len(wins[s])):
            to_ahead(s, c).wait_send()
            to_mate(s, c).wait_send()
            for copy in to_rims(s, c):
                copy.wait_send()
    for c in range(len(wins[2])):
        for copy in to_edges(c):
            copy.wait_send()
    for c in range(len(wins[3])):
        if wins[3][c][1] > wins[3][c][0]:
            to_out(c).wait()


def fused(sizes, latent, gain_one, conv_one, gain_two, conv_two, up_weight):
    _, height, width, channels = latent.shape
    growth = up_weight.shape[3]
    first = windows(width, 48, 32)
    second = settled(first, width, 16)
    third = settled(second, width, 16)
    fourth = settled(third, width, 8)
    wins = (first, second, third, fourth)
    count = len(first)
    dma = pltpu.SemaphoreType.DMA
    bf16, f32 = jnp.bfloat16, jnp.float32
    return pl.pallas_call(
        functools.partial(kernel, sizes, wins),
        out_shape=jax.ShapeDtypeStruct((1, 2 * height, 2 * width, growth), bf16),
        in_specs=[
            pl.BlockSpec(memory_space=pl.ANY),
            pl.BlockSpec(memory_space=pltpu.VMEM),
            pl.BlockSpec(memory_space=pltpu.VMEM),
            pl.BlockSpec(memory_space=pl.ANY),
            pl.BlockSpec(memory_space=pl.ANY),
            pl.BlockSpec(memory_space=pl.ANY),
        ],
        out_specs=pl.BlockSpec(memory_space=pl.ANY),
        scratch_shapes=[
            pltpu.VMEM((height, width, channels), bf16),
            pltpu.VMEM((2, 3, 3, 3, channels, channels), bf16),
            pltpu.VMEM((3, 3, channels, growth), bf16),
            pltpu.VMEM((2, 2 * channels, 4 * growth), bf16),
            pltpu.VMEM((2, 3, height + 2, width, channels), bf16),
            pltpu.VMEM((height + 2, width, channels), bf16),
            pltpu.VMEM((3, height, width + 2 * PAD, channels), f32),
            pltpu.VMEM((2, height, width + 2 * PAD, 4 * growth), f32),
            pltpu.VMEM((2 * width, growth), f32),
            pltpu.VMEM((2 * height, 2 * width, growth), bf16),
            dma((8,)),
            dma((count,)),
            dma((2, count)),
            dma((2, count)),
            dma((2, count)),
            dma((2, count)),
            dma((2, count, 2)),
            dma((2, count, 2)),
            dma((count, 2)),
            dma((count, 2)),
        ],
        compiler_params=pltpu.CompilerParams(
            collective_id=0, has_side_effects=True, vmem_limit_bytes=56 * 1024 * 1024
        ),
    )(
        latent,
        gain_one.reshape(1, channels),
        gain_two.reshape(1, channels),
        conv_one,
        conv_two,
        up_weight,
    )


def solution(mesh):
    sizes = (mesh.shape["tm"], mesh.shape["rows"])
    placed = (P("tm", "rows", None, None), P(), P(), P(), P(), P())
    return jax.shard_map(
        functools.partial(fused, sizes),
        mesh=mesh,
        in_specs=placed,
        out_specs=P("tm", "rows", None, None),
        check_vma=False,
    )
```

```python
import functools

import jax
import jax.numpy as jnp
from jax import lax
from jax.experimental import pallas as pl
from jax.experimental.pallas import tpu as pltpu
from jax.sharding import PartitionSpec as P

MESH = pl.DeviceIdType.MESH
PAD = 8


def norm_silu(values, scales):
    mean_sq = jnp.mean(values * values, axis=-1, keepdims=True)
    u = values * lax.rsqrt(mean_sq + 1e-06) * scales
    return 0.5 * u * (1.0 + jnp.tanh(0.5 * u))


def kernel(
    sizes,
    latent,
    gain_one,
    gain_two,
    conv_one,
    conv_two,
    up_weight,
    out,
    lat,
    weights,
    up_raw,
    up_mat,
    held,
    block,
    sums,
    up_sums,
    woven,
    packed,
    load_sem,
    out_sem,
    frame_send,
    frame_recv,
    pair_send,
    pair_recv,
    rim_send,
    rim_recv,
    edge_send,
    edge_recv,
):
    frames, bands = sizes
    height, width, channels = lat.shape
    growth = up_raw.shape[3]
    pairs = height // 2
    tm, rw = lax.axis_index("tm"), lax.axis_index("rows")
    odd = lax.rem(tm, 2)
    mate = (tm + 1 - 2 * odd, rw)
    ahead = (lax.rem(tm + 2, frames), rw)
    behind = (lax.rem(tm + frames - 2, frames), rw)
    above = (tm, lax.rem(rw + bands - 1, bands))
    below = (tm, lax.rem(rw + 1, bands))

    def slot(row):
        return 2 * (row + 1) if row < pairs else 2 * (height - row) + 1

    def rows_of(k):
        return (k, height - 1 - k)

    loads = [pltpu.make_async_copy(latent.at[0], lat, load_sem.at[0])]
    for stage, conv in enumerate((conv_one, conv_two)):
        for e in range(3):
            loads.append(
                pltpu.make_async_copy(
                    conv.at[:, :, e], weights.at[stage, e], load_sem.at[1 + 3 * stage + e]
                )
            )
    loads.append(pltpu.make_async_copy(up_weight, up_raw, load_sem.at[7]))
    for load in loads:
        load.start()

    barrier = pltpu.get_barrier_semaphore()
    for peer in (behind, mate, above, below):
        pl.semaphore_signal(barrier, inc=1, device_id=peer, device_id_type=MESH)

    def remote(src, dst, send, recv, peer):
        return pltpu.make_async_remote_copy(
            src_ref=src, dst_ref=dst, send_sem=send, recv_sem=recv, device_id=peer, device_id_type=MESH
        )

    def to_ahead(s, k):
        both = pl.ds(2 * k + 2, 2)
        return remote(
            held.at[s, 2, both],
            held.at[s, 0, both],
            frame_send.at[s, k],
            frame_recv.at[s, k],
            ahead,
        )

    def to_mate(s, k):
        both = pl.ds(2 * k + 2, 2)
        return remote(
            held.at[s, 2 - 2 * odd, both],
            held.at[s, 1, both],
            pair_send.at[s, k],
            pair_recv.at[s, k],
            mate,
        )

    def to_rims(s, a):
        return [
            remote(
                held.at[s, a, mine],
                held.at[s, a, theirs],
                rim_send.at[s, a, i],
                rim_recv.at[s, a, i],
                peer,
            )
            for i, (mine, theirs, peer) in enumerate(((2, 1, above), (3, 0, below)))
        ]

    def to_edges():
        return [
            remote(block.at[mine], block.at[theirs], edge_send.at[i], edge_recv.at[i], peer)
            for i, (mine, theirs, peer) in enumerate(((2, 1, above), (3, 0, below)))
        ]

    def to_out(k):
        return [
            pltpu.make_async_copy(
                packed.at[pl.ds(2 * row, 2)], out.at[0, pl.ds(2 * row, 2)], out_sem.at[k, i]
            )
            for i, row in enumerate(rows_of(k))
        ]

    def start(copies):
        for copy in copies:
            copy.start()

    def send_own(s, k):
        to_ahead(s, k).start()
        if k == 0:
            start(to_rims(s, 2))

    def take_frame(s, k):
        to_ahead(s, k).wait_recv()

        @pl.when(tm < 2)
        def _():
            held[s, 0, 2 * k + 2 : 2 * k + 4] = jnp.zeros((2, width, channels), held.dtype)

        to_mate(s, k).start()
        if k == 0:
            start(to_rims(s, 0))

    def take_pair(s, k):
        to_mate(s, k).wait_recv()
        if k == 0:
            start(to_rims(s, 1))

    def take_rims(s):
        for a in range(3):
            for copy in to_rims(s, a):
                copy.wait_recv()
        blank = jnp.zeros((3, width, channels), held.dtype)

        @pl.when(rw == 0)
        def _():
            held[s, :, 0] = blank

        @pl.when(rw == bands - 1)
        def _():
            held[s, :, 1] = blank

    def multiply(s, k):
        left = jnp.concatenate(
            [
                jnp.concatenate([held[s, a, slot(row + b - 1)] for row in rows_of(k)], axis=0)
                for a in range(3)
                for b in range(3)
            ],
            axis=1,
        )
        for e in range(3):
            term = jnp.dot(
                left,
                weights[s, e].reshape(9 * channels, channels),
                preferred_element_type=jnp.float32,
            )
            sums[e, :, PAD : PAD + width] = term.reshape(2, width, channels)

    def total(i, lo, n):
        return (
            sums[0, i, PAD + lo - 1 : PAD + lo - 1 + n]
            + sums[1, i, PAD + lo : PAD + lo + n]
            + sums[2, i, PAD + lo + 1 : PAD + lo + 1 + n]
        )

    def settle_one(k):
        for i in range(2):
            for lo in range(0, width, 32):
                value = norm_silu(total(i, lo, 32), gain_two[...])
                held[1, 2, 2 * k + 2 + i, lo : lo + 32] = value.astype(held.dtype)
        send_own(1, k)

    def settle_two(k):
        for i, row in enumerate(rows_of(k)):
            for lo in range(0, width, 32):
                value = lat[row, lo : lo + 32].astype(jnp.float32) + total(i, lo, 32)
                block[2 * k + 2 + i, lo : lo + 32] = value.astype(block.dtype)
        if k == 0:
            start(to_edges())

    def take_edges():
        for copy in to_edges():
            copy.wait_recv()
        blank = jnp.zeros((width, channels), block.dtype)

        @pl.when(rw == 0)
        def _():
            block[0] = blank

        @pl.when(rw == bands - 1)
        def _():
            block[1] = blank

    def upsample(k):
        g = growth
        for p in range(2):
            left = jnp.concatenate(
                [
                    jnp.concatenate([block[slot(row + p + d - 1)] for row in rows_of(k)], axis=0)
                    for d in range(2)
                ],
                axis=1,
            )
            term = jnp.dot(left, up_mat[p], preferred_element_type=jnp.float32)
            up_sums[p, :, PAD : PAD + width] = term.reshape(2, width, 4 * g)
        for p in range(2):
            for i, row in enumerate(rows_of(k)):
                even = (
                    up_sums[p, i, PAD - 1 : PAD - 1 + width, 0:g]
                    + up_sums[p, i, PAD : PAD + width, g : 2 * g]
                )
                odds = (
                    up_sums[p, i, PAD : PAD + width, 2 * g : 3 * g]
                    + up_sums[p, i, PAD + 1 : PAD + 1 + width, 3 * g : 4 * g]
                )
                woven[p, i, pl.ds(0, width, stride=2), :] = even
                woven[p, i, pl.ds(1, width, stride=2), :] = odds
                packed[2 * row + p] = woven[p, i].astype(packed.dtype)
        start(to_out(k))

    loads[0].wait()
    pl.semaphore_wait(barrier, 4)
    for k in range(pairs):
        for i, row in enumerate(rows_of(k)):
            for lo in range(0, width, 32):
                value = norm_silu(lat[row, lo : lo + 32].astype(jnp.float32), gain_one[...])
                held[0, 2, 2 * k + 2 + i, lo : lo + 32] = value.astype(held.dtype)
        send_own(0, k)

    sums[0, :, 0:PAD] = jnp.zeros((2, PAD, channels), jnp.float32)
    sums[2, :, PAD + width :] = jnp.zeros((2, PAD, channels), jnp.float32)
    for p in range(2):
        up_sums[p, :, 0:PAD, 0:growth] = jnp.zeros((2, PAD, growth), jnp.float32)
        up_sums[p, :, PAD + width :, 3 * growth :] = jnp.zeros((2, PAD, growth), jnp.float32)
    loads[7].wait()
    for p, groups in enumerate((((0,), (1, 2)), ((0, 1), (2,)))):
        for d, group in enumerate(groups):
            col = [sum(up_raw[b, e].astype(jnp.float32) for b in group) for e in range(3)]
            parts = (col[0], col[1] + col[2], col[0] + col[1], col[2])
            for j, part in enumerate(parts):
                up_mat[p, d * channels : (d + 1) * channels, j * growth : (j + 1) * growth] = part.astype(
                    up_mat.dtype
                )

    take_frame(0, 0)
    take_pair(0, 0)
    take_frame(0, 1)
    for load in loads[1:4]:
        load.wait()
    take_pair(0, 1)
    take_rims(0)
    for k in range(pairs):
        multiply(0, k)
        if k + 2 < pairs:
            take_frame(0, k + 2)
        if k == pairs - 1:
            take_frame(1, 0)
        settle_one(k)
        if k + 2 < pairs:
            take_pair(0, k + 2)

    take_pair(1, 0)
    take_frame(1, 1)
    for load in loads[4:7]:
        load.wait()
    take_pair(1, 1)
    take_rims(1)
    for k in range(pairs):
        multiply(1, k)
        if k + 2 < pairs:
            take_frame(1, k + 2)
        settle_two(k)
        if k == 1:
            take_edges()
        if k >= 1:
            upsample(k - 1)
        if k + 2 < pairs:
            take_pair(1, k + 2)
    upsample(pairs - 1)

    for s in range(2):
        for k in range(pairs):
            to_ahead(s, k).wait_send()
            to_mate(s, k).wait_send()
        for a in range(3):
            for copy in to_rims(s, a):
                copy.wait_send()
    for copy in to_edges():
        copy.wait_send()
    for k in range(pairs):
        for copy in to_out(k):
            copy.wait()


def fused(sizes, latent, gain_one, conv_one, gain_two, conv_two, up_weight):
    _, height, width, channels = latent.shape
    growth = up_weight.shape[3]
    pairs = height // 2
    dma = pltpu.SemaphoreType.DMA
    bf16, f32 = jnp.bfloat16, jnp.float32
    return pl.pallas_call(
        functools.partial(kernel, sizes),
        out_shape=jax.ShapeDtypeStruct((1, 2 * height, 2 * width, growth), bf16),
        in_specs=[
            pl.BlockSpec(memory_space=pl.ANY),
            pl.BlockSpec(memory_space=pltpu.VMEM),
            pl.BlockSpec(memory_space=pltpu.VMEM),
            pl.BlockSpec(memory_space=pl.ANY),
            pl.BlockSpec(memory_space=pl.ANY),
            pl.BlockSpec(memory_space=pl.ANY),
        ],
        out_specs=pl.BlockSpec(memory_space=pl.ANY),
        scratch_shapes=[
            pltpu.VMEM((height, width, channels), bf16),
            pltpu.VMEM((2, 3, 3, 3, channels, channels), bf16),
            pltpu.VMEM((3, 3, channels, growth), bf16),
            pltpu.VMEM((2, 2 * channels, 4 * growth), bf16),
            pltpu.VMEM((2, 3, height + 2, width, channels), bf16),
            pltpu.VMEM((height + 2, width, channels), bf16),
            pltpu.VMEM((3, 2, width + 2 * PAD, channels), f32),
            pltpu.VMEM((2, 2, width + 2 * PAD, 4 * growth), f32),
            pltpu.VMEM((2, 2, 2 * width, growth), f32),
            pltpu.VMEM((2 * height, 2 * width, growth), bf16),
            dma((8,)),
            dma((pairs, 2)),
            dma((2, pairs)),
            dma((2, pairs)),
            dma((2, pairs)),
            dma((2, pairs)),
            dma((2, 3, 2)),
            dma((2, 3, 2)),
            dma((2,)),
            dma((2,)),
        ],
        compiler_params=pltpu.CompilerParams(
            collective_id=0, has_side_effects=True, vmem_limit_bytes=56 * 1024 * 1024
        ),
    )(
        latent,
        gain_one.reshape(1, channels),
        gain_two.reshape(1, channels),
        conv_one,
        conv_two,
        up_weight,
    )


def solution(mesh):
    sizes = (mesh.shape["tm"], mesh.shape["rows"])
    placed = (P("tm", "rows", None, None), P(), P(), P(), P(), P())
    return jax.shard_map(
        functools.partial(fused, sizes),
        mesh=mesh,
        in_specs=placed,
        out_specs=P("tm", "rows", None, None),
        check_vma=False,
    )
```

```python
import functools

import jax
import jax.numpy as jnp
from jax import lax
from jax.experimental import pallas as pl
from jax.experimental.pallas import tpu as pltpu
from jax.sharding import PartitionSpec as P

MESH = pl.DeviceIdType.MESH
PAD = 8


def norm_silu(values, scales):
    mean_sq = jnp.mean(values * values, axis=-1, keepdims=True)
    u = values * lax.rsqrt(mean_sq + 1e-06) * scales
    return 0.5 * u * (1.0 + jnp.tanh(0.5 * u))


def kernel(
    sizes,
    latent,
    gain_one,
    gain_two,
    conv_one,
    conv_two,
    up_weight,
    out,
    lat,
    weights,
    up_raw,
    up_mat,
    held,
    block,
    sums,
    up_sums,
    woven,
    load_sem,
    frame_send,
    frame_recv,
    pair_send,
    pair_recv,
    rim_send,
    rim_recv,
    edge_send,
    edge_recv,
):
    frames, bands = sizes
    height, width, channels = lat.shape
    growth = up_raw.shape[3]
    pairs = height // 2
    tm, rw = lax.axis_index("tm"), lax.axis_index("rows")
    odd = lax.rem(tm, 2)
    mate = (tm + 1 - 2 * odd, rw)
    ahead = (lax.rem(tm + 2, frames), rw)
    behind = (lax.rem(tm + frames - 2, frames), rw)
    above = (tm, lax.rem(rw + bands - 1, bands))
    below = (tm, lax.rem(rw + 1, bands))

    def slot(row):
        return 2 * (row + 1) if row < pairs else 2 * (height - row) + 1

    def rows_of(k):
        return (k, height - 1 - k)

    loads = [pltpu.make_async_copy(latent.at[0], lat, load_sem.at[0])]
    for stage, conv in enumerate((conv_one, conv_two)):
        for e in range(3):
            loads.append(
                pltpu.make_async_copy(
                    conv.at[:, :, e], weights.at[stage, e], load_sem.at[1 + 3 * stage + e]
                )
            )
    loads.append(pltpu.make_async_copy(up_weight, up_raw, load_sem.at[7]))
    for load in loads:
        load.start()

    barrier = pltpu.get_barrier_semaphore()
    for peer in (behind, mate, above, below):
        pl.semaphore_signal(barrier, inc=1, device_id=peer, device_id_type=MESH)

    def remote(src, dst, send, recv, peer):
        return pltpu.make_async_remote_copy(
            src_ref=src, dst_ref=dst, send_sem=send, recv_sem=recv, device_id=peer, device_id_type=MESH
        )

    def to_ahead(s, k):
        both = pl.ds(2 * k + 2, 2)
        return remote(
            held.at[s, 2, both],
            held.at[s, 0, both],
            frame_send.at[s, k],
            frame_recv.at[s, k],
            ahead,
        )

    def to_mate(s, k):
        both = pl.ds(2 * k + 2, 2)
        return remote(
            held.at[s, 2 - 2 * odd, both],
            held.at[s, 1, both],
            pair_send.at[s, k],
            pair_recv.at[s, k],
            mate,
        )

    def to_rims(s, a):
        return [
            remote(
                held.at[s, a, mine],
                held.at[s, a, theirs],
                rim_send.at[s, a, i],
                rim_recv.at[s, a, i],
                peer,
            )
            for i, (mine, theirs, peer) in enumerate(((2, 1, above), (3, 0, below)))
        ]

    def to_edges():
        return [
            remote(block.at[mine], block.at[theirs], edge_send.at[i], edge_recv.at[i], peer)
            for i, (mine, theirs, peer) in enumerate(((2, 1, above), (3, 0, below)))
        ]

    def to_out(k):
        return [
            pltpu.make_async_copy(
                packed.at[pl.ds(2 * row, 2)], out.at[0, pl.ds(2 * row, 2)], out_sem.at[k, i]
            )
            for i, row in enumerate(rows_of(k))
        ]

    def start(copies):
        for copy in copies:
            copy.start()

    def send_own(s, k):
        to_ahead(s, k).start()

        @pl.when(odd == 0)
        def _():
            to_mate(s, k).start()

        if k == 0:
            start(to_rims(s, 2))

    def take_frame(s, k):
        to_ahead(s, k).wait_recv()

        @pl.when(tm < 2)
        def _():
            held[s, 0, 2 * k + 2 : 2 * k + 4] = jnp.zeros((2, width, channels), held.dtype)

        @pl.when(odd == 1)
        def _():
            to_mate(s, k).start()

        if k == 0:
            start(to_rims(s, 0))

    def take_pair(s, k):
        to_mate(s, k).wait_recv()
        if k == 0:
            start(to_rims(s, 1))

    def take_rims(s, lo, hi):
        for a in range(lo, hi):
            for copy in to_rims(s, a):
                copy.wait_recv()
        blank = jnp.zeros((hi - lo, width, channels), held.dtype)

        @pl.when(rw == 0)
        def _():
            held[s, lo:hi, 0] = blank

        @pl.when(rw == bands - 1)
        def _():
            held[s, lo:hi, 1] = blank

    def multiply(s, ks, lo, hi, add):
        rows = [row for k in ks for row in rows_of(k)]
        left = jnp.concatenate(
            [
                jnp.concatenate([held[s, a, slot(row + b - 1)] for row in rows], axis=0)
                for a in range(lo, hi)
                for b in range(3)
            ],
            axis=1,
        )
        here = pl.ds(2 * ks[0], len(rows))
        for e in range(3):
            term = jnp.dot(
                left,
                weights[s, e, lo:hi].reshape(3 * (hi - lo) * channels, channels),
                preferred_element_type=jnp.float32,
            ).reshape(len(rows), width, channels)
            if add:
                term = term + sums[e, here, PAD : PAD + width]
            sums[e, here, PAD : PAD + width] = term

    def total(i, lo, n):
        return (
            sums[0, i, PAD + lo - 1 : PAD + lo - 1 + n]
            + sums[1, i, PAD + lo : PAD + lo + n]
            + sums[2, i, PAD + lo + 1 : PAD + lo + 1 + n]
        )

    def settle_one(k):
        for i in range(2):
            for lo in range(0, width, 32):
                value = norm_silu(total(2 * k + i, lo, 32), gain_two[...])
                held[1, 2, 2 * k + 2 + i, lo : lo + 32] = value.astype(held.dtype)
        send_own(1, k)

    def settle_two(k):
        for i, row in enumerate(rows_of(k)):
            for lo in range(0, width, 32):
                value = lat[row, lo : lo + 32].astype(jnp.float32) + total(2 * k + i, lo, 32)
                block[2 * k + 2 + i, lo : lo + 32] = value.astype(block.dtype)
        if k == 0:
            start(to_edges())

    def take_edges():
        for copy in to_edges():
            copy.wait_recv()
        blank = jnp.zeros((width, channels), block.dtype)

        @pl.when(rw == 0)
        def _():
            block[0] = blank

        @pl.when(rw == bands - 1)
        def _():
            block[1] = blank

    def upsample(k):
        g = growth
        for p in range(2):
            left = jnp.concatenate(
                [
                    jnp.concatenate([block[slot(row + p + d - 1)] for row in rows_of(k)], axis=0)
                    for d in range(2)
                ],
                axis=1,
            )
            term = jnp.dot(left, up_mat[p], preferred_element_type=jnp.float32)
            up_sums[p, :, PAD : PAD + width] = term.reshape(2, width, 4 * g)
        for p in range(2):
            for i, row in enumerate(rows_of(k)):
                even = (
                    up_sums[p, i, PAD - 1 : PAD - 1 + width, 0:g]
                    + up_sums[p, i, PAD : PAD + width, g : 2 * g]
                )
                odds = (
                    up_sums[p, i, PAD : PAD + width, 2 * g : 3 * g]
                    + up_sums[p, i, PAD + 1 : PAD + 1 + width, 3 * g : 4 * g]
                )
                woven[p, i, pl.ds(0, width, stride=2), :] = even
                woven[p, i, pl.ds(1, width, stride=2), :] = odds
                out[0, 2 * row + p] = woven[p, i].astype(out.dtype)

    loads[0].wait()
    pl.semaphore_wait(barrier, 4)
    for k in range(pairs):
        for i, row in enumerate(rows_of(k)):
            for lo in range(0, width, 32):
                value = norm_silu(lat[row, lo : lo + 32].astype(jnp.float32), gain_one[...])
                held[0, 2, 2 * k + 2 + i, lo : lo + 32] = value.astype(held.dtype)
        send_own(0, k)

    sums[0, :, 0:PAD] = jnp.zeros((height, PAD, channels), jnp.float32)
    sums[2, :, PAD + width :] = jnp.zeros((height, PAD, channels), jnp.float32)
    for p in range(2):
        up_sums[p, :, 0:PAD, 0:growth] = jnp.zeros((2, PAD, growth), jnp.float32)
        up_sums[p, :, PAD + width :, 3 * growth :] = jnp.zeros((2, PAD, growth), jnp.float32)
    loads[7].wait()
    for p, groups in enumerate((((0,), (1, 2)), ((0, 1), (2,)))):
        for d, group in enumerate(groups):
            col = [sum(up_raw[b, e].astype(jnp.float32) for b in group) for e in range(3)]
            parts = (col[0], col[1] + col[2], col[0] + col[1], col[2])
            for j, part in enumerate(parts):
                up_mat[p, d * channels : (d + 1) * channels, j * growth : (j + 1) * growth] = part.astype(
                    up_mat.dtype
                )

    for load in loads[1:4]:
        load.wait()
    take_rims(0, 2, 3)
    multiply(0, (0, 1), 2, 3, False)
    multiply(0, (2, 3), 2, 3, False)
    take_frame(0, 0)
    take_pair(0, 0)
    take_frame(0, 1)
    take_pair(0, 1)
    take_rims(0, 0, 2)
    multiply(0, (0,), 0, 2, True)
    settle_one(0)
    take_frame(0, 2)
    take_pair(0, 2)
    multiply(0, (1,), 0, 2, True)
    settle_one(1)
    take_frame(0, 3)
    take_pair(0, 3)
    multiply(0, (2, 3), 0, 2, True)
    settle_one(2)
    settle_one(3)

    for load in loads[4:7]:
        load.wait()
    take_frame(1, 0)
    take_pair(1, 0)
    take_rims(1, 2, 3)
    multiply(1, (0, 1), 2, 3, False)
    multiply(1, (2, 3), 2, 3, False)
    take_frame(1, 1)
    take_pair(1, 1)
    take_rims(1, 0, 2)
    multiply(1, (0,), 0, 2, True)
    settle_two(0)
    take_frame(1, 2)
    take_pair(1, 2)
    multiply(1, (1,), 0, 2, True)
    settle_two(1)
    take_frame(1, 3)
    take_edges()
    upsample(0)
    take_pair(1, 3)
    multiply(1, (2, 3), 0, 2, True)
    settle_two(2)
    upsample(1)
    settle_two(3)
    upsample(2)
    upsample(3)

    for s in range(2):
        for k in range(pairs):
            to_ahead(s, k).wait_send()
            to_mate(s, k).wait_send()
        for a in range(3):
            for copy in to_rims(s, a):
                copy.wait_send()
    for copy in to_edges():
        copy.wait_send()


def fused(sizes, latent, gain_one, conv_one, gain_two, conv_two, up_weight):
    _, height, width, channels = latent.shape
    growth = up_weight.shape[3]
    pairs = height // 2
    dma = pltpu.SemaphoreType.DMA
    bf16, f32 = jnp.bfloat16, jnp.float32
    return pl.pallas_call(
        functools.partial(kernel, sizes),
        out_shape=pltpu.VMEM((1, 2 * height, 2 * width, growth), bf16),
        in_specs=[
            pl.BlockSpec(memory_space=pl.ANY),
            pl.BlockSpec(memory_space=pltpu.VMEM),
            pl.BlockSpec(memory_space=pltpu.VMEM),
            pl.BlockSpec(memory_space=pl.ANY),
            pl.BlockSpec(memory_space=pl.ANY),
            pl.BlockSpec(memory_space=pl.ANY),
        ],
        out_specs=pl.BlockSpec(memory_space=pltpu.VMEM),
        scratch_shapes=[
            pltpu.VMEM((height, width, channels), bf16),
            pltpu.VMEM((2, 3, 3, 3, channels, channels), bf16),
            pltpu.VMEM((3, 3, channels, growth), bf16),
            pltpu.VMEM((2, 2 * channels, 4 * growth), bf16),
            pltpu.VMEM((2, 3, height + 2, width, channels), bf16),
            pltpu.VMEM((height + 2, width, channels), bf16),
            pltpu.VMEM((3, height, width + 2 * PAD, channels), f32),
            pltpu.VMEM((2, 2, width + 2 * PAD, 4 * growth), f32),
            pltpu.VMEM((2, 2, 2 * width, growth), f32),
            dma((8,)),
            dma((2, pairs)),
            dma((2, pairs)),
            dma((2, pairs)),
            dma((2, pairs)),
            dma((2, 3, 2)),
            dma((2, 3, 2)),
            dma((2,)),
            dma((2,)),
        ],
        compiler_params=pltpu.CompilerParams(
            collective_id=0, has_side_effects=True, vmem_limit_bytes=56 * 1024 * 1024
        ),
    )(
        latent,
        gain_one.reshape(1, channels),
        gain_two.reshape(1, channels),
        conv_one,
        conv_two,
        up_weight,
    )


def solution(mesh):
    sizes = (mesh.shape["tm"], mesh.shape["rows"])
    placed = (P("tm", "rows", None, None), P(), P(), P(), P(), P())
    return jax.shard_map(
        functools.partial(fused, sizes),
        mesh=mesh,
        in_specs=placed,
        out_specs=P("tm", "rows", None, None),
        check_vma=False,
    )
```

```python
import functools

import jax
import jax.numpy as jnp
from jax import lax
from jax.experimental import pallas as pl
from jax.experimental.pallas import tpu as pltpu
from jax.sharding import PartitionSpec as P

MESH = pl.DeviceIdType.MESH
PAD = 8


def norm_silu(values, scales):
    mean_sq = jnp.mean(values * values, axis=-1, keepdims=True)
    u = values * lax.rsqrt(mean_sq + 1e-06) * scales
    return 0.5 * u * (1.0 + jnp.tanh(0.5 * u))


def kernel(
    sizes,
    latent,
    gain_one,
    gain_two,
    conv_one,
    conv_two,
    up_weight,
    out,
    lat,
    weights,
    up_raw,
    up_mat,
    held,
    block,
    sums,
    up_sums,
    woven,
    load_sem,
    frame_send,
    frame_recv,
    pair_send,
    pair_recv,
    rim_send,
    rim_recv,
    edge_send,
    edge_recv,
):
    frames, bands = sizes
    height, width, channels = lat.shape
    growth = up_raw.shape[3]
    pairs = height // 2
    tm, rw = lax.axis_index("tm"), lax.axis_index("rows")
    odd = lax.rem(tm, 2)
    mate = (tm + 1 - 2 * odd, rw)
    ahead = (lax.rem(tm + 2, frames), rw)
    behind = (lax.rem(tm + frames - 2, frames), rw)
    above = (tm, lax.rem(rw + bands - 1, bands))
    below = (tm, lax.rem(rw + 1, bands))
    has_ahead, has_behind = tm < frames - 2, tm >= 2
    has_above, has_below = rw > 0, rw < bands - 1

    def slot(row):
        return 2 * (row + 1) if row < pairs else 2 * (height - row) + 1

    def rows_of(k):
        return (k, height - 1 - k)

    loads = [pltpu.make_async_copy(latent.at[0], lat, load_sem.at[0])]
    for stage, conv in enumerate((conv_one, conv_two)):
        for e in range(3):
            loads.append(
                pltpu.make_async_copy(
                    conv.at[:, :, e], weights.at[stage, e], load_sem.at[1 + 3 * stage + e]
                )
            )
    loads.append(pltpu.make_async_copy(up_weight, up_raw, load_sem.at[7]))
    for load in loads:
        load.start()

    barrier = pltpu.get_barrier_semaphore()
    pl.semaphore_signal(barrier, inc=1, device_id=mate, device_id_type=MESH)
    for ok, peer in ((has_behind, behind), (has_above, above), (has_below, below)):

        @pl.when(ok)
        def _(peer=peer):
            pl.semaphore_signal(barrier, inc=1, device_id=peer, device_id_type=MESH)

    def remote(src, dst, send, recv, peer):
        return pltpu.make_async_remote_copy(
            src_ref=src, dst_ref=dst, send_sem=send, recv_sem=recv, device_id=peer, device_id_type=MESH
        )

    def to_ahead(s, k):
        both = pl.ds(2 * k + 2, 2)
        return remote(
            held.at[s, 2, both],
            held.at[s, 0, both],
            frame_send.at[s, k],
            frame_recv.at[s, k],
            ahead,
        )

    def to_mate(s, k):
        both = pl.ds(2 * k + 2, 2)
        return remote(
            held.at[s, 2 - 2 * odd, both],
            held.at[s, 1, both],
            pair_send.at[s, k],
            pair_recv.at[s, k],
            mate,
        )

    def to_rims(s, a):
        return [
            remote(
                held.at[s, a, mine],
                held.at[s, a, theirs],
                rim_send.at[s, a, i],
                rim_recv.at[s, a, i],
                peer,
            )
            for i, (mine, theirs, peer) in enumerate(((2, 1, above), (3, 0, below)))
        ]

    def to_edges():
        return [
            remote(block.at[mine], block.at[theirs], edge_send.at[i], edge_recv.at[i], peer)
            for i, (mine, theirs, peer) in enumerate(((2, 1, above), (3, 0, below)))
        ]

    def to_out(k):
        return [
            pltpu.make_async_copy(
                packed.at[pl.ds(2 * row, 2)], out.at[0, pl.ds(2 * row, 2)], out_sem.at[k, i]
            )
            for i, row in enumerate(rows_of(k))
        ]

    def start(copies):
        for copy in copies:
            copy.start()

    def to_rows(copies, act):
        for copy, ok in zip(copies, (has_above, has_below)):

            @pl.when(ok)
            def _(copy=copy):
                act(copy)

    def send_rows(copies):
        to_rows(copies, lambda copy: copy.start())

    def drain_rows(copies):
        to_rows(copies, lambda copy: copy.wait_send())

    def take_rows(copies):
        to_rows(copies[::-1], lambda copy: copy.wait_recv())

    def send_own(s, k):
        @pl.when(has_ahead)
        def _():
            to_ahead(s, k).start()

        @pl.when(odd == 0)
        def _():
            to_mate(s, k).start()

        if k == 0:
            send_rows(to_rims(s, 2))

    def take_frame(s, k):
        @pl.when(has_behind)
        def _():
            to_ahead(s, k).wait_recv()

        @pl.when(odd == 1)
        def _():
            to_mate(s, k).start()

        if k == 0:
            send_rows(to_rims(s, 0))

    def take_pair(s, k):
        to_mate(s, k).wait_recv()
        if k == 0:
            send_rows(to_rims(s, 1))

    def take_rims(s, lo, hi):
        for a in range(lo, hi):
            take_rows(to_rims(s, a))

    def multiply(s, ks, lo, hi, add):
        rows = [row for k in ks for row in rows_of(k)]
        left = jnp.concatenate(
            [
                jnp.concatenate([held[s, a, slot(row + b - 1)] for row in rows], axis=0)
                for a in range(lo, hi)
                for b in range(3)
            ],
            axis=1,
        )
        here = pl.ds(2 * ks[0], len(rows))
        for e in range(3):
            term = jnp.dot(
                left,
                weights[s, e, lo:hi].reshape(3 * (hi - lo) * channels, channels),
                preferred_element_type=jnp.float32,
            ).reshape(len(rows), width, channels)
            if add:
                term = term + sums[e, here, PAD : PAD + width]
            sums[e, here, PAD : PAD + width] = term

    def total(i, lo, n):
        return (
            sums[0, i, PAD + lo - 1 : PAD + lo - 1 + n]
            + sums[1, i, PAD + lo : PAD + lo + n]
            + sums[2, i, PAD + lo + 1 : PAD + lo + 1 + n]
        )

    def settle_one(k):
        for i in range(2):
            for lo in range(0, width, 32):
                value = norm_silu(total(2 * k + i, lo, 32), gain_two[...])
                held[1, 2, 2 * k + 2 + i, lo : lo + 32] = value.astype(held.dtype)
        send_own(1, k)

    def settle_two(k):
        for i, row in enumerate(rows_of(k)):
            for lo in range(0, width, 32):
                value = lat[row, lo : lo + 32].astype(jnp.float32) + total(2 * k + i, lo, 32)
                block[2 * k + 2 + i, lo : lo + 32] = value.astype(block.dtype)
        if k == 0:
            send_rows(to_edges())

    def upsample(*ks):
        g = growth
        rows = [row for k in ks for row in rows_of(k)]
        n = len(rows)
        for p in range(2):
            left = jnp.concatenate(
                [
                    jnp.concatenate([block[slot(row + p + d - 1)] for row in rows], axis=0)
                    for d in range(2)
                ],
                axis=1,
            )
            term = jnp.dot(left, up_mat[p], preferred_element_type=jnp.float32)
            up_sums[p, 0:n, PAD : PAD + width] = term.reshape(n, width, 4 * g)
        for p in range(2):
            for i, row in enumerate(rows):
                even = (
                    up_sums[p, i, PAD - 1 : PAD - 1 + width, 0:g]
                    + up_sums[p, i, PAD : PAD + width, g : 2 * g]
                )
                odds = (
                    up_sums[p, i, PAD : PAD + width, 2 * g : 3 * g]
                    + up_sums[p, i, PAD + 1 : PAD + 1 + width, 3 * g : 4 * g]
                )
                woven[p, i, pl.ds(0, width, stride=2), :] = even
                woven[p, i, pl.ds(1, width, stride=2), :] = odds
                out[0, 2 * row + p] = woven[p, i].astype(out.dtype)

    loads[0].wait()
    peers = 1 + sum(ok.astype(jnp.int32) for ok in (has_ahead, has_above, has_below))
    pl.semaphore_wait(barrier, peers)
    for k in range(pairs):
        for i, row in enumerate(rows_of(k)):
            for lo in range(0, width, 32):
                value = norm_silu(lat[row, lo : lo + 32].astype(jnp.float32), gain_one[...])
                held[0, 2, 2 * k + 2 + i, lo : lo + 32] = value.astype(held.dtype)
        send_own(0, k)

    for ok, place in ((has_above, 0), (has_below, 1)):

        @pl.when(jnp.logical_not(ok))
        def _(place=place):
            held[:, :, place] = jnp.zeros((2, 3, width, channels), held.dtype)
            block[place] = jnp.zeros((width, channels), block.dtype)

    @pl.when(jnp.logical_not(has_behind))
    def _():
        held[:, 0, 2:] = jnp.zeros((2, height, width, channels), held.dtype)

    sums[0, :, 0:PAD] = jnp.zeros((height, PAD, channels), jnp.float32)
    sums[2, :, PAD + width :] = jnp.zeros((height, PAD, channels), jnp.float32)
    for p in range(2):
        up_sums[p, :, 0:PAD, 0:growth] = jnp.zeros((6, PAD, growth), jnp.float32)
        up_sums[p, :, PAD + width :, 3 * growth :] = jnp.zeros((6, PAD, growth), jnp.float32)
    loads[7].wait()
    for p, groups in enumerate((((0,), (1, 2)), ((0, 1), (2,)))):
        for d, group in enumerate(groups):
            col = [sum(up_raw[b, e].astype(jnp.float32) for b in group) for e in range(3)]
            parts = (col[0], col[1] + col[2], col[0] + col[1], col[2])
            for j, part in enumerate(parts):
                up_mat[p, d * channels : (d + 1) * channels, j * growth : (j + 1) * growth] = part.astype(
                    up_mat.dtype
                )

    for load in loads[1:4]:
        load.wait()
    take_rims(0, 2, 3)
    multiply(0, (0, 1), 2, 3, False)
    multiply(0, (2, 3), 2, 3, False)
    take_frame(0, 0)
    take_pair(0, 0)
    take_frame(0, 1)
    take_rims(0, 0, 1)
    multiply(0, (0,), 0, 1, True)
    take_pair(0, 1)
    take_rims(0, 1, 2)
    multiply(0, (0,), 1, 2, True)
    settle_one(0)
    take_frame(0, 2)
    multiply(0, (1,), 0, 1, True)
    take_pair(0, 2)
    multiply(0, (1,), 1, 2, True)
    settle_one(1)
    take_frame(0, 3)
    multiply(0, (2, 3), 0, 1, True)
    take_pair(0, 3)
    multiply(0, (2, 3), 1, 2, True)
    settle_one(2)
    settle_one(3)

    for load in loads[4:7]:
        load.wait()
    take_frame(1, 0)
    take_pair(1, 0)
    take_rims(1, 2, 3)
    multiply(1, (0, 1), 2, 3, False)
    multiply(1, (2, 3), 2, 3, False)
    take_frame(1, 1)
    take_pair(1, 1)
    take_rims(1, 0, 2)
    multiply(1, (0,), 0, 2, True)
    settle_two(0)
    take_frame(1, 2)
    take_pair(1, 2)
    multiply(1, (1,), 0, 2, True)
    settle_two(1)
    take_frame(1, 3)
    multiply(1, (2, 3), 0, 1, True)
    take_rows(to_edges())
    upsample(0)
    take_pair(1, 3)
    multiply(1, (2, 3), 1, 2, True)
    settle_two(2)
    settle_two(3)
    upsample(1, 2, 3)

    for s in range(2):
        for k in range(pairs):

            @pl.when(has_ahead)
            def _(s=s, k=k):
                to_ahead(s, k).wait_send()

            to_mate(s, k).wait_send()
        for a in range(3):
            drain_rows(to_rims(s, a))
    drain_rows(to_edges())


def fused(sizes, latent, gain_one, conv_one, gain_two, conv_two, up_weight):
    _, height, width, channels = latent.shape
    growth = up_weight.shape[3]
    pairs = height // 2
    dma = pltpu.SemaphoreType.DMA
    bf16, f32 = jnp.bfloat16, jnp.float32
    return pl.pallas_call(
        functools.partial(kernel, sizes),
        out_shape=pltpu.VMEM((1, 2 * height, 2 * width, growth), bf16),
        in_specs=[
            pl.BlockSpec(memory_space=pl.ANY),
            pl.BlockSpec(memory_space=pltpu.VMEM),
            pl.BlockSpec(memory_space=pltpu.VMEM),
            pl.BlockSpec(memory_space=pl.ANY),
            pl.BlockSpec(memory_space=pl.ANY),
            pl.BlockSpec(memory_space=pl.ANY),
        ],
        out_specs=pl.BlockSpec(memory_space=pltpu.VMEM),
        scratch_shapes=[
            pltpu.VMEM((height, width, channels), bf16),
            pltpu.VMEM((2, 3, 3, 3, channels, channels), bf16),
            pltpu.VMEM((3, 3, channels, growth), bf16),
            pltpu.VMEM((2, 2 * channels, 4 * growth), bf16),
            pltpu.VMEM((2, 3, height + 2, width, channels), bf16),
            pltpu.VMEM((height + 2, width, channels), bf16),
            pltpu.VMEM((3, height, width + 2 * PAD, channels), f32),
            pltpu.VMEM((2, 6, width + 2 * PAD, 4 * growth), f32),
            pltpu.VMEM((2, 6, 2 * width, growth), f32),
            dma((8,)),
            dma((2, pairs)),
            dma((2, pairs)),
            dma((2, pairs)),
            dma((2, pairs)),
            dma((2, 3, 2)),
            dma((2, 3, 2)),
            dma((2,)),
            dma((2,)),
        ],
        compiler_params=pltpu.CompilerParams(
            collective_id=0, has_side_effects=True, vmem_limit_bytes=56 * 1024 * 1024
        ),
    )(
        latent,
        gain_one.reshape(1, channels),
        gain_two.reshape(1, channels),
        conv_one,
        conv_two,
        up_weight,
    )


def solution(mesh):
    sizes = (mesh.shape["tm"], mesh.shape["rows"])
    placed = (P("tm", "rows", None, None), P(), P(), P(), P(), P())
    return jax.shard_map(
        functools.partial(fused, sizes),
        mesh=mesh,
        in_specs=placed,
        out_specs=P("tm", "rows", None, None),
        check_vma=False,
    )
```

```python
import functools

import jax
import jax.numpy as jnp
from jax import lax
from jax.experimental import pallas as pl
from jax.experimental.pallas import tpu as pltpu
from jax.sharding import PartitionSpec as P

MESH = pl.DeviceIdType.MESH
PAD = 8


def norm_silu(values, scales):
    mean_sq = jnp.mean(values * values, axis=-1, keepdims=True)
    u = values * lax.rsqrt(mean_sq + 1e-06) * scales
    return 0.5 * u * (1.0 + jnp.tanh(0.5 * u))


def kernel(
    sizes,
    latent,
    gain_one,
    gain_two,
    conv_one,
    conv_two,
    up_weight,
    out,
    lat,
    weights,
    up_raw,
    up_mat,
    held,
    block,
    sums,
    up_sums,
    woven,
    load_sem,
    frame_send,
    frame_recv,
    pair_send,
    pair_recv,
    rim_send,
    rim_recv,
    edge_send,
    edge_recv,
):
    frames, bands = sizes
    height, width, channels = lat.shape
    growth = up_raw.shape[3]
    pairs = height // 2
    tm, rw = lax.axis_index("tm"), lax.axis_index("rows")
    odd = lax.rem(tm, 2)
    mate = (tm + 1 - 2 * odd, rw)
    ahead = (lax.rem(tm + 2, frames), rw)
    behind = (lax.rem(tm + frames - 2, frames), rw)
    above = (tm, lax.rem(rw + bands - 1, bands))
    below = (tm, lax.rem(rw + 1, bands))
    has_ahead, has_behind = tm < frames - 2, tm >= 2
    has_above, has_below = rw > 0, rw < bands - 1

    def slot(row):
        return 2 * (row + 1) if row < pairs else 2 * (height - row) + 1

    def rows_of(k):
        return (k, height - 1 - k)

    loads = [pltpu.make_async_copy(latent.at[0], lat, load_sem.at[0])]
    for stage, conv in enumerate((conv_one, conv_two)):
        for e in range(3):
            loads.append(
                pltpu.make_async_copy(
                    conv.at[:, :, e], weights.at[stage, e], load_sem.at[1 + 3 * stage + e]
                )
            )
    loads.append(pltpu.make_async_copy(up_weight, up_raw, load_sem.at[7]))
    for load in loads:
        load.start()

    barrier = pltpu.get_barrier_semaphore()
    pl.semaphore_signal(barrier, inc=1, device_id=mate, device_id_type=MESH)
    for ok, peer in ((has_behind, behind), (has_above, above), (has_below, below)):

        @pl.when(ok)
        def _(peer=peer):
            pl.semaphore_signal(barrier, inc=1, device_id=peer, device_id_type=MESH)

    def remote(src, dst, send, recv, peer):
        return pltpu.make_async_remote_copy(
            src_ref=src, dst_ref=dst, send_sem=send, recv_sem=recv, device_id=peer, device_id_type=MESH
        )

    def to_ahead(s, k):
        both = pl.ds(2 * k + 2, 2)
        return remote(
            held.at[s, 2, both],
            held.at[s, 0, both],
            frame_send.at[s, k],
            frame_recv.at[s, k],
            ahead,
        )

    def to_mate(s, k):
        both = pl.ds(2 * k + 2, 2)
        return remote(
            held.at[s, 2 - 2 * odd, both],
            held.at[s, 1, both],
            pair_send.at[s, k],
            pair_recv.at[s, k],
            mate,
        )

    def to_rims(s, a):
        return [
            remote(
                held.at[s, a, mine],
                held.at[s, a, theirs],
                rim_send.at[s, a, i],
                rim_recv.at[s, a, i],
                peer,
            )
            for i, (mine, theirs, peer) in enumerate(((2, 1, above), (3, 0, below)))
        ]

    def to_edges():
        return [
            remote(block.at[mine], block.at[theirs], edge_send.at[i], edge_recv.at[i], peer)
            for i, (mine, theirs, peer) in enumerate(((2, 1, above), (3, 0, below)))
        ]

    def to_out(k):
        return [
            pltpu.make_async_copy(
                packed.at[pl.ds(2 * row, 2)], out.at[0, pl.ds(2 * row, 2)], out_sem.at[k, i]
            )
            for i, row in enumerate(rows_of(k))
        ]

    def start(copies):
        for copy in copies:
            copy.start()

    def to_rows(copies, act):
        for copy, ok in zip(copies, (has_above, has_below)):

            @pl.when(ok)
            def _(copy=copy):
                act(copy)

    def send_rows(copies):
        to_rows(copies, lambda copy: copy.start())

    def drain_rows(copies):
        to_rows(copies, lambda copy: copy.wait_send())

    def take_rows(copies):
        to_rows(copies[::-1], lambda copy: copy.wait_recv())

    def send_own(s, k):
        @pl.when(has_ahead)
        def _():
            to_ahead(s, k).start()

        @pl.when(odd == 0)
        def _():
            to_mate(s, k).start()

        if k == 0:
            send_rows(to_rims(s, 2))

    def take_frame(s, k):
        @pl.when(has_behind)
        def _():
            to_ahead(s, k).wait_recv()

        @pl.when(odd == 1)
        def _():
            to_mate(s, k).start()

        if k == 0:
            send_rows(to_rims(s, 0))

    def take_pair(s, k):
        to_mate(s, k).wait_recv()
        if k == 0:
            send_rows(to_rims(s, 1))

    def take_rims(s, lo, hi):
        for a in range(lo, hi):
            take_rows(to_rims(s, a))

    def multiply(s, ks, lo, hi, add):
        rows = [row for k in ks for row in rows_of(k)]
        left = jnp.concatenate(
            [
                jnp.concatenate([held[s, a, slot(row + b - 1)] for row in rows], axis=0)
                for a in range(lo, hi)
                for b in range(3)
            ],
            axis=1,
        )
        here = pl.ds(2 * ks[0], len(rows))
        for e in range(3):
            term = jnp.dot(
                left,
                weights[s, e, lo:hi].reshape(3 * (hi - lo) * channels, channels),
                preferred_element_type=jnp.float32,
            ).reshape(len(rows), width, channels)
            if add:
                term = term + sums[e, here, PAD : PAD + width]
            sums[e, here, PAD : PAD + width] = term

    def total(i, lo, n):
        return (
            sums[0, i, PAD + lo - 1 : PAD + lo - 1 + n]
            + sums[1, i, PAD + lo : PAD + lo + n]
            + sums[2, i, PAD + lo + 1 : PAD + lo + 1 + n]
        )

    def settle_one(k):
        for i in range(2):
            for lo in range(0, width, 32):
                value = norm_silu(total(2 * k + i, lo, 32), gain_two[...])
                held[1, 2, 2 * k + 2 + i, lo : lo + 32] = value.astype(held.dtype)
        send_own(1, k)

    def settle_two(k):
        for i, row in enumerate(rows_of(k)):
            for lo in range(0, width, 32):
                value = lat[row, lo : lo + 32].astype(jnp.float32) + total(2 * k + i, lo, 32)
                block[2 * k + 2 + i, lo : lo + 32] = value.astype(block.dtype)
        if k == 0:
            send_rows(to_edges())

    def upsample(*ks):
        g = growth
        rows = [row for k in ks for row in rows_of(k)]
        n = len(rows)
        for p in range(2):
            left = jnp.concatenate(
                [
                    jnp.concatenate([block[slot(row + p + d - 1)] for row in rows], axis=0)
                    for d in range(2)
                ],
                axis=1,
            )
            term = jnp.dot(left, up_mat[p], preferred_element_type=jnp.float32)
            up_sums[p, 0:n, PAD : PAD + width] = term.reshape(n, width, 4 * g)
        for p in range(2):
            for i, row in enumerate(rows):
                even = (
                    up_sums[p, i, PAD - 1 : PAD - 1 + width, 0:g]
                    + up_sums[p, i, PAD : PAD + width, g : 2 * g]
                )
                odds = (
                    up_sums[p, i, PAD : PAD + width, 2 * g : 3 * g]
                    + up_sums[p, i, PAD + 1 : PAD + 1 + width, 3 * g : 4 * g]
                )
                woven[p, i, pl.ds(0, width, stride=2), :] = even
                woven[p, i, pl.ds(1, width, stride=2), :] = odds
                out[0, 2 * row + p] = woven[p, i].astype(out.dtype)

    loads[0].wait()
    peers = 1 + sum(ok.astype(jnp.int32) for ok in (has_ahead, has_above, has_below))
    pl.semaphore_wait(barrier, peers)
    for k in range(pairs):
        for i, row in enumerate(rows_of(k)):
            for lo in range(0, width, 32):
                value = norm_silu(lat[row, lo : lo + 32].astype(jnp.float32), gain_one[...])
                held[0, 2, 2 * k + 2 + i, lo : lo + 32] = value.astype(held.dtype)
        send_own(0, k)

    for ok, place in ((has_above, 0), (has_below, 1)):

        @pl.when(jnp.logical_not(ok))
        def _(place=place):
            held[:, :, place] = jnp.zeros((2, 3, width, channels), held.dtype)
            block[place] = jnp.zeros((width, channels), block.dtype)

    @pl.when(jnp.logical_not(has_behind))
    def _():
        held[:, 0, 2:] = jnp.zeros((2, height, width, channels), held.dtype)

    sums[0, :, 0:PAD] = jnp.zeros((height, PAD, channels), jnp.float32)
    sums[2, :, PAD + width :] = jnp.zeros((height, PAD, channels), jnp.float32)
    for p in range(2):
        up_sums[p, :, 0:PAD, 0:growth] = jnp.zeros((8, PAD, growth), jnp.float32)
        up_sums[p, :, PAD + width :, 3 * growth :] = jnp.zeros((8, PAD, growth), jnp.float32)
    loads[7].wait()
    for p, groups in enumerate((((0,), (1, 2)), ((0, 1), (2,)))):
        for d, group in enumerate(groups):
            col = [sum(up_raw[b, e].astype(jnp.float32) for b in group) for e in range(3)]
            parts = (col[0], col[1] + col[2], col[0] + col[1], col[2])
            for j, part in enumerate(parts):
                up_mat[p, d * channels : (d + 1) * channels, j * growth : (j + 1) * growth] = part.astype(
                    up_mat.dtype
                )

    for load in loads[1:4]:
        load.wait()
    take_rims(0, 2, 3)
    multiply(0, (0, 1), 2, 3, False)
    multiply(0, (2, 3), 2, 3, False)
    take_frame(0, 0)
    take_pair(0, 0)
    take_frame(0, 1)
    take_rims(0, 0, 1)
    multiply(0, (0,), 0, 1, True)
    take_pair(0, 1)
    take_rims(0, 1, 2)
    multiply(0, (0,), 1, 2, True)
    settle_one(0)
    take_frame(0, 2)
    multiply(0, (1,), 0, 1, True)
    take_pair(0, 2)
    multiply(0, (1,), 1, 2, True)
    settle_one(1)
    take_frame(0, 3)
    multiply(0, (2, 3), 0, 1, True)
    take_pair(0, 3)
    multiply(0, (2, 3), 1, 2, True)
    settle_one(2)
    settle_one(3)

    for load in loads[4:7]:
        load.wait()
    take_frame(1, 0)
    take_pair(1, 0)
    take_rims(1, 2, 3)
    multiply(1, (0, 1), 2, 3, False)
    multiply(1, (2, 3), 2, 3, False)
    take_frame(1, 1)
    take_rims(1, 0, 1)
    multiply(1, (0,), 0, 1, True)
    take_pair(1, 1)
    take_rims(1, 1, 2)
    multiply(1, (0,), 1, 2, True)
    settle_two(0)
    take_frame(1, 2)
    multiply(1, (1,), 0, 1, True)
    take_pair(1, 2)
    multiply(1, (1,), 1, 2, True)
    settle_two(1)
    take_frame(1, 3)
    multiply(1, (2, 3), 0, 1, True)
    take_pair(1, 3)
    multiply(1, (2, 3), 1, 2, True)
    settle_two(2)
    settle_two(3)
    upsample(1, 2, 3)
    take_rows(to_edges())
    upsample(0)

    for s in range(2):
        for k in range(pairs):

            @pl.when(has_ahead)
            def _(s=s, k=k):
                to_ahead(s, k).wait_send()

            to_mate(s, k).wait_send()
        for a in range(3):
            drain_rows(to_rims(s, a))
    drain_rows(to_edges())


def fused(sizes, latent, gain_one, conv_one, gain_two, conv_two, up_weight):
    _, height, width, channels = latent.shape
    growth = up_weight.shape[3]
    pairs = height // 2
    dma = pltpu.SemaphoreType.DMA
    bf16, f32 = jnp.bfloat16, jnp.float32
    return pl.pallas_call(
        functools.partial(kernel, sizes),
        out_shape=pltpu.VMEM((1, 2 * height, 2 * width, growth), bf16),
        in_specs=[
            pl.BlockSpec(memory_space=pl.ANY),
            pl.BlockSpec(memory_space=pltpu.VMEM),
            pl.BlockSpec(memory_space=pltpu.VMEM),
            pl.BlockSpec(memory_space=pl.ANY),
            pl.BlockSpec(memory_space=pl.ANY),
            pl.BlockSpec(memory_space=pl.ANY),
        ],
        out_specs=pl.BlockSpec(memory_space=pltpu.VMEM),
        scratch_shapes=[
            pltpu.VMEM((height, width, channels), bf16),
            pltpu.VMEM((2, 3, 3, 3, channels, channels), bf16),
            pltpu.VMEM((3, 3, channels, growth), bf16),
            pltpu.VMEM((2, 2 * channels, 4 * growth), bf16),
            pltpu.VMEM((2, 3, height + 2, width, channels), bf16),
            pltpu.VMEM((height + 2, width, channels), bf16),
            pltpu.VMEM((3, height, width + 2 * PAD, channels), f32),
            pltpu.VMEM((2, 8, width + 2 * PAD, 4 * growth), f32),
            pltpu.VMEM((2, 8, 2 * width, growth), f32),
            dma((8,)),
            dma((2, pairs)),
            dma((2, pairs)),
            dma((2, pairs)),
            dma((2, pairs)),
            dma((2, 3, 2)),
            dma((2, 3, 2)),
            dma((2,)),
            dma((2,)),
        ],
        compiler_params=pltpu.CompilerParams(
            collective_id=0, has_side_effects=True, vmem_limit_bytes=56 * 1024 * 1024
        ),
    )(
        latent,
        gain_one.reshape(1, channels),
        gain_two.reshape(1, channels),
        conv_one,
        conv_two,
        up_weight,
    )


def solution(mesh):
    sizes = (mesh.shape["tm"], mesh.shape["rows"])
    placed = (P("tm", "rows", None, None), P(), P(), P(), P(), P())
    return jax.shard_map(
        functools.partial(fused, sizes),
        mesh=mesh,
        in_specs=placed,
        out_specs=P("tm", "rows", None, None),
        check_vma=False,
    )
```

```python
import functools

import jax
import jax.numpy as jnp
from jax import lax
from jax.experimental import pallas as pl
from jax.experimental.pallas import tpu as pltpu
from jax.sharding import PartitionSpec as P

MESH = pl.DeviceIdType.MESH
PAD = 8
RING = 8


def norm_silu(values, scales):
    mean_sq = jnp.mean(values * values, axis=-1, keepdims=True)
    u = values * lax.rsqrt(mean_sq + 1e-06) * scales
    return 0.5 * u * (1.0 + jnp.tanh(0.5 * u))


def kernel(
    sizes,
    latent,
    gain_one,
    gain_two,
    conv_one,
    conv_two,
    up_weight,
    out,
    lat,
    weights,
    up_raw,
    up_mat,
    held,
    block,
    sums,
    up_sums,
    woven,
    load_sem,
    frame_send,
    frame_recv,
    pair_send,
    pair_recv,
    rim_send,
    rim_recv,
    edge_send,
    edge_recv,
    passing,
    relay_send,
    relay_recv,
):
    frames, bands = sizes
    height, width, channels = lat.shape
    growth = up_raw.shape[3]
    pairs = height // 2
    tm, rw = lax.axis_index("tm"), lax.axis_index("rows")
    odd = lax.rem(tm, 2)
    mate = (tm + 1 - 2 * odd, rw)
    ahead = (lax.rem(tm + 2, frames), rw)
    behind = (lax.rem(tm + frames - 2, frames), rw)
    above = (tm, lax.rem(rw + bands - 1, bands))
    below = (tm, lax.rem(rw + 1, bands))
    has_ahead, has_behind = tm < frames - 2, tm >= 2
    turn = lax.rem(tm, RING)
    down = (tm - turn + lax.rem(turn + RING - 2, RING), rw)
    up = (tm - turn + lax.rem(turn + 2, RING), rw)
    leaves, enters = turn // 2 == 1, turn // 2 == 0
    far_out = (lax.rem(tm + RING - 2, frames), rw)
    far_in = (lax.rem(tm + frames - RING + 2, frames), rw)
    has_out = jnp.logical_and(leaves, tm < frames - RING)
    has_in = jnp.logical_and(enters, tm >= RING)
    has_above, has_below = rw > 0, rw < bands - 1

    def slot(row):
        return 2 * (row + 1) if row < pairs else 2 * (height - row) + 1

    def rows_of(k):
        return (k, height - 1 - k)

    loads = [pltpu.make_async_copy(latent.at[0], lat, load_sem.at[0])]
    for stage, conv in enumerate((conv_one, conv_two)):
        for e in range(3):
            loads.append(
                pltpu.make_async_copy(
                    conv.at[:, :, e], weights.at[stage, e], load_sem.at[1 + 3 * stage + e]
                )
            )
    loads.append(pltpu.make_async_copy(up_weight, up_raw, load_sem.at[7]))
    for load in loads:
        load.start()

    barrier = pltpu.get_barrier_semaphore()
    pl.semaphore_signal(barrier, inc=1, device_id=mate, device_id_type=MESH)
    pl.semaphore_signal(barrier, inc=1, device_id=up, device_id_type=MESH)
    for ok, peer in (
        (has_behind, behind),
        (has_in, far_in),
        (has_above, above),
        (has_below, below),
    ):

        @pl.when(ok)
        def _(peer=peer):
            pl.semaphore_signal(barrier, inc=1, device_id=peer, device_id_type=MESH)

    def remote(src, dst, send, recv, peer):
        return pltpu.make_async_remote_copy(
            src_ref=src, dst_ref=dst, send_sem=send, recv_sem=recv, device_id=peer, device_id_type=MESH
        )

    def relay(step, peer):
        last = height + 1
        src = (held.at[0, 2, last], passing.at[0], passing.at[1])[step]
        dst = (passing.at[0], passing.at[1], held.at[0, 0, last])[step]
        return remote(src, dst, relay_send.at[step], relay_recv.at[step], peer)

    def to_ahead(s, k):
        both = pl.ds(2 * k + 2, 1 if s == 0 and k == pairs - 1 else 2)
        return remote(
            held.at[s, 2, both],
            held.at[s, 0, both],
            frame_send.at[s, k],
            frame_recv.at[s, k],
            ahead,
        )

    def to_mate(s, k):
        both = pl.ds(2 * k + 2, 2)
        return remote(
            held.at[s, 2 - 2 * odd, both],
            held.at[s, 1, both],
            pair_send.at[s, k],
            pair_recv.at[s, k],
            mate,
        )

    def to_rims(s, a):
        return [
            remote(
                held.at[s, a, mine],
                held.at[s, a, theirs],
                rim_send.at[s, a, i],
                rim_recv.at[s, a, i],
                peer,
            )
            for i, (mine, theirs, peer) in enumerate(((2, 1, above), (3, 0, below)))
        ]

    def to_edges():
        return [
            remote(block.at[mine], block.at[theirs], edge_send.at[i], edge_recv.at[i], peer)
            for i, (mine, theirs, peer) in enumerate(((2, 1, above), (3, 0, below)))
        ]

    def to_out(k):
        return [
            pltpu.make_async_copy(
                packed.at[pl.ds(2 * row, 2)], out.at[0, pl.ds(2 * row, 2)], out_sem.at[k, i]
            )
            for i, row in enumerate(rows_of(k))
        ]

    def start(copies):
        for copy in copies:
            copy.start()

    def to_rows(copies, act):
        for copy, ok in zip(copies, (has_above, has_below)):

            @pl.when(ok)
            def _(copy=copy):
                act(copy)

    def send_rows(copies):
        to_rows(copies, lambda copy: copy.start())

    def drain_rows(copies):
        to_rows(copies, lambda copy: copy.wait_send())

    def take_rows(copies):
        to_rows(copies[::-1], lambda copy: copy.wait_recv())

    def when(ok, act):
        @pl.when(ok)
        def _():
            act()

    def pass_out(act):
        when(jnp.logical_not(leaves), lambda: act(relay(2, down)))
        when(has_out, lambda: act(relay(2, far_out)))

    def send_own(s, k):
        @pl.when(has_ahead)
        def _():
            to_ahead(s, k).start()

        @pl.when(odd == 0)
        def _():
            to_mate(s, k).start()

        if k == 0:
            send_rows(to_rims(s, 2))

    def take_frame(s, k):
        @pl.when(has_behind)
        def _():
            to_ahead(s, k).wait_recv()
            if s == 0 and k == pairs - 1:
                relay(2, down).wait_recv()

        @pl.when(odd == 1)
        def _():
            to_mate(s, k).start()

        if k == 0:
            send_rows(to_rims(s, 0))

    def take_pair(s, k):
        to_mate(s, k).wait_recv()
        if k == 0:
            send_rows(to_rims(s, 1))

    def take_rims(s, lo, hi):
        for a in range(lo, hi):
            take_rows(to_rims(s, a))

    def multiply(s, ks, lo, hi, add):
        rows = [row for k in ks for row in rows_of(k)]
        left = jnp.concatenate(
            [
                jnp.concatenate([held[s, a, slot(row + b - 1)] for row in rows], axis=0)
                for a in range(lo, hi)
                for b in range(3)
            ],
            axis=1,
        )
        here = pl.ds(2 * ks[0], len(rows))
        for e in range(3):
            term = jnp.dot(
                left,
                weights[s, e, lo:hi].reshape(3 * (hi - lo) * channels, channels),
                preferred_element_type=jnp.float32,
            ).reshape(len(rows), width, channels)
            if add:
                term = term + sums[e, here, PAD : PAD + width]
            sums[e, here, PAD : PAD + width] = term

    def total(i, lo, n):
        return (
            sums[0, i, PAD + lo - 1 : PAD + lo - 1 + n]
            + sums[1, i, PAD + lo : PAD + lo + n]
            + sums[2, i, PAD + lo + 1 : PAD + lo + 1 + n]
        )

    def settle_one(k):
        for i in range(2):
            for lo in range(0, width, 32):
                value = norm_silu(total(2 * k + i, lo, 32), gain_two[...])
                held[1, 2, 2 * k + 2 + i, lo : lo + 32] = value.astype(held.dtype)
        send_own(1, k)

    def settle_two(k):
        for i, row in enumerate(rows_of(k)):
            for lo in range(0, width, 32):
                value = lat[row, lo : lo + 32].astype(jnp.float32) + total(2 * k + i, lo, 32)
                block[2 * k + 2 + i, lo : lo + 32] = value.astype(block.dtype)
        if k == 0:
            send_rows(to_edges())

    def upsample(*ks):
        g = growth
        rows = [row for k in ks for row in rows_of(k)]
        n = len(rows)
        for p in range(2):
            left = jnp.concatenate(
                [
                    jnp.concatenate([block[slot(row + p + d - 1)] for row in rows], axis=0)
                    for d in range(2)
                ],
                axis=1,
            )
            term = jnp.dot(left, up_mat[p], preferred_element_type=jnp.float32)
            up_sums[p, 0:n, PAD : PAD + width] = term.reshape(n, width, 4 * g)
        for p in range(2):
            for i, row in enumerate(rows):
                even = (
                    up_sums[p, i, PAD - 1 : PAD - 1 + width, 0:g]
                    + up_sums[p, i, PAD : PAD + width, g : 2 * g]
                )
                odds = (
                    up_sums[p, i, PAD : PAD + width, 2 * g : 3 * g]
                    + up_sums[p, i, PAD + 1 : PAD + 1 + width, 3 * g : 4 * g]
                )
                woven[p, i, pl.ds(0, width, stride=2), :] = even
                woven[p, i, pl.ds(1, width, stride=2), :] = odds
                out[0, 2 * row + p] = woven[p, i].astype(out.dtype)

    loads[0].wait()
    peers = 2 + sum(ok.astype(jnp.int32) for ok in (has_ahead, has_out, has_above, has_below))
    pl.semaphore_wait(barrier, peers)
    for k in (0, 3, 1, 2):
        for i, row in enumerate(rows_of(k)):
            for lo in range(0, width, 32):
                value = norm_silu(lat[row, lo : lo + 32].astype(jnp.float32), gain_one[...])
                held[0, 2, 2 * k + 2 + i, lo : lo + 32] = value.astype(held.dtype)
        if k == pairs - 1:
            relay(0, down).start()
        else:
            send_own(0, k)
    send_own(0, pairs - 1)

    for ok, place in ((has_above, 0), (has_below, 1)):

        @pl.when(jnp.logical_not(ok))
        def _(place=place):
            held[:, :, place] = jnp.zeros((2, 3, width, channels), held.dtype)
            block[place] = jnp.zeros((width, channels), block.dtype)

    @pl.when(jnp.logical_not(has_behind))
    def _():
        held[:, 0, 2:] = jnp.zeros((2, height, width, channels), held.dtype)

    sums[0, :, 0:PAD] = jnp.zeros((height, PAD, channels), jnp.float32)
    sums[2, :, PAD + width :] = jnp.zeros((height, PAD, channels), jnp.float32)
    for p in range(2):
        up_sums[p, :, 0:PAD, 0:growth] = jnp.zeros((8, PAD, growth), jnp.float32)
        up_sums[p, :, PAD + width :, 3 * growth :] = jnp.zeros((8, PAD, growth), jnp.float32)
    loads[7].wait()
    for p, groups in enumerate((((0,), (1, 2)), ((0, 1), (2,)))):
        for d, group in enumerate(groups):
            col = [sum(up_raw[b, e].astype(jnp.float32) for b in group) for e in range(3)]
            parts = (col[0], col[1] + col[2], col[0] + col[1], col[2])
            for j, part in enumerate(parts):
                up_mat[p, d * channels : (d + 1) * channels, j * growth : (j + 1) * growth] = part.astype(
                    up_mat.dtype
                )

    for load in loads[1:4]:
        load.wait()
    take_rims(0, 2, 3)
    multiply(0, (0, 1), 2, 3, False)
    multiply(0, (2, 3), 2, 3, False)
    relay(0, down).wait_recv()
    relay(1, down).start()
    take_frame(0, 0)
    take_pair(0, 0)
    take_frame(0, 1)
    take_rims(0, 0, 1)
    multiply(0, (0,), 0, 1, True)
    relay(1, down).wait_recv()
    pass_out(lambda copy: copy.start())
    take_pair(0, 1)
    take_rims(0, 1, 2)
    multiply(0, (0,), 1, 2, True)
    settle_one(0)
    take_frame(0, 2)
    multiply(0, (1,), 0, 1, True)
    take_pair(0, 2)
    multiply(0, (1,), 1, 2, True)
    settle_one(1)
    take_frame(0, 3)
    multiply(0, (2, 3), 0, 1, True)
    take_pair(0, 3)
    multiply(0, (2, 3), 1, 2, True)
    settle_one(2)
    settle_one(3)

    for load in loads[4:7]:
        load.wait()
    take_frame(1, 0)
    take_pair(1, 0)
    take_rims(1, 2, 3)
    multiply(1, (0, 1), 2, 3, False)
    multiply(1, (2, 3), 2, 3, False)
    take_frame(1, 1)
    take_rims(1, 0, 1)
    multiply(1, (0,), 0, 1, True)
    take_pair(1, 1)
    take_rims(1, 1, 2)
    multiply(1, (0,), 1, 2, True)
    settle_two(0)
    take_frame(1, 2)
    multiply(1, (1,), 0, 1, True)
    take_pair(1, 2)
    multiply(1, (1,), 1, 2, True)
    settle_two(1)
    take_frame(1, 3)
    multiply(1, (2, 3), 0, 1, True)
    take_pair(1, 3)
    multiply(1, (2, 3), 1, 2, True)
    settle_two(2)
    settle_two(3)
    upsample(1, 2, 3)
    take_rows(to_edges())
    upsample(0)

    relay(0, down).wait_send()
    relay(1, down).wait_send()
    pass_out(lambda copy: copy.wait_send())
    for s in range(2):
        for k in range(pairs):

            @pl.when(has_ahead)
            def _(s=s, k=k):
                to_ahead(s, k).wait_send()

            to_mate(s, k).wait_send()
        for a in range(3):
            drain_rows(to_rims(s, a))
    drain_rows(to_edges())


def fused(sizes, latent, gain_one, conv_one, gain_two, conv_two, up_weight):
    _, height, width, channels = latent.shape
    growth = up_weight.shape[3]
    pairs = height // 2
    dma = pltpu.SemaphoreType.DMA
    bf16, f32 = jnp.bfloat16, jnp.float32
    return pl.pallas_call(
        functools.partial(kernel, sizes),
        out_shape=pltpu.VMEM((1, 2 * height, 2 * width, growth), bf16),
        in_specs=[
            pl.BlockSpec(memory_space=pl.ANY),
            pl.BlockSpec(memory_space=pltpu.VMEM),
            pl.BlockSpec(memory_space=pltpu.VMEM),
            pl.BlockSpec(memory_space=pl.ANY),
            pl.BlockSpec(memory_space=pl.ANY),
            pl.BlockSpec(memory_space=pl.ANY),
        ],
        out_specs=pl.BlockSpec(memory_space=pltpu.VMEM),
        scratch_shapes=[
            pltpu.VMEM((height, width, channels), bf16),
            pltpu.VMEM((2, 3, 3, 3, channels, channels), bf16),
            pltpu.VMEM((3, 3, channels, growth), bf16),
            pltpu.VMEM((2, 2 * channels, 4 * growth), bf16),
            pltpu.VMEM((2, 3, height + 2, width, channels), bf16),
            pltpu.VMEM((height + 2, width, channels), bf16),
            pltpu.VMEM((3, height, width + 2 * PAD, channels), f32),
            pltpu.VMEM((2, 8, width + 2 * PAD, 4 * growth), f32),
            pltpu.VMEM((2, 8, 2 * width, growth), f32),
            dma((8,)),
            dma((2, pairs)),
            dma((2, pairs)),
            dma((2, pairs)),
            dma((2, pairs)),
            dma((2, 3, 2)),
            dma((2, 3, 2)),
            dma((2,)),
            dma((2,)),
            pltpu.VMEM((2, width, channels), bf16),
            dma((3,)),
            dma((3,)),
        ],
        compiler_params=pltpu.CompilerParams(
            collective_id=0, has_side_effects=True, vmem_limit_bytes=56 * 1024 * 1024
        ),
    )(
        latent,
        gain_one.reshape(1, channels),
        gain_two.reshape(1, channels),
        conv_one,
        conv_two,
        up_weight,
    )


def solution(mesh):
    sizes = (mesh.shape["tm"], mesh.shape["rows"])
    placed = (P("tm", "rows", None, None), P(), P(), P(), P(), P())
    return jax.shard_map(
        functools.partial(fused, sizes),
        mesh=mesh,
        in_specs=placed,
        out_specs=P("tm", "rows", None, None),
        check_vma=False,
    )
```
